32 devices in a mesh: harm: 2 (over x), space: 16 (over z, y, core).
Axes of the slice: x: 2, y: 2, z: 4, core: 2. Of those that a mesh axis runs over, the one named last changes fastest.
Arguments:
- rhs_field: float32 [64, 4096], P('harm', 'space'), may hold values from -14 to 14
- neighbors: int32 [8, 4096], P(None, 'space'), may hold values from 0 to 4095, as said below
- nu_mean: float32 [8, 4096], P(None, 'space'), may hold values from 0.5 to 4
- nu_ripple: float32 [64, 8, 4096], P(None, None, 'space'), may hold values from -0.24 to 0.24
- mass_coeff: float32 [4096], P('space'), may hold values from 0.5 to 2
- eddy_coeff: float32 [4096], P('space'), may hold values from 0.25 to 2
Outputs:
- correction: float32 [64, 4096], P('harm', 'space')
- residual: float32 [64, 4096], P('harm', 'space')
The draws below stay inside these ranges and needn't reach their ends.
Inputs may be any that keep to these rules, and one draw needn't show every extreme that they name: neighbors[d, n] is a node at most 64 places from n in the node order closed into a loop (node 4095 lies next to node 0), or n itself for an unused slot; slot 0 is always used, and some entry lies 64 places away in each direction.
All inputs are finite; a program needn't handle non-finite values.
Results may differ from the reference program's by a relative error of at most 0.0003.
Values sent between devices are 32-bit elements; how exact they have to be, the bound alone decides.
A program may use at most 64 MiB of HBM per device.

```python
import math
import jax
import jax.numpy as jnp
from jax import lax

H = 64
DEG = 8
IF = 64
ITERS = 8
NODES = 4096


def draw_rhs_field(key, part):
    k_noise, k_rows, k_cols = jax.random.split(key, 3)
    position = jnp.arange(NODES, dtype=jnp.float32)
    column_scale = jnp.exp(jnp.log(3.0) * position / max(NODES - 1, 1) + jax.random.uniform(k_cols, (NODES,), minval=0.0, maxval=jnp.log(3.0)))
    noise = jnp.clip(jax.random.normal(k_noise, (H, NODES)), -4.0, 4.0)
    row_scale = jnp.exp(jax.random.uniform(k_rows, (H, 1), minval=jnp.log(0.25), maxval=0.0))
    return (noise * row_scale * column_scale[None, :] / 3.0).astype(jnp.float32)


def draw_neighbors(key, part):
    k_step, k_live = jax.random.split(key)
    position = jnp.arange(NODES, dtype=jnp.int32)
    stride = jax.random.randint(k_step, (DEG, NODES), -IF, IF + 1)
    live_slots = jax.random.randint(k_live, (1, NODES), 2, DEG + 1)
    slot_index = jnp.arange(DEG, dtype=jnp.int32)[:, None]
    stride = jnp.where(slot_index < live_slots, stride, 0)
    stride = stride.at[0, 0].set(IF).at[0, 1].set(-IF)
    return jnp.mod(position[None, :] + stride, NODES).astype(jnp.int32)


def levels(stream_key, shape, cuts, low, high):
    factor_of, own = 1.0, jax.random.fold_in(stream_key, 6)
    for dim, parts in cuts:
        steps = jnp.exp(jax.random.uniform(jax.random.fold_in(own, dim), (parts,), jnp.float32, low / len(cuts), high / len(cuts)))
        factor_of = factor_of * jnp.repeat(steps, shape[dim] // parts).reshape([-1 if axis == dim else 1 for axis in range(len(shape))])
    return factor_of


def gaussian(key, extent, spread, limit, cuts=(), kind=jnp.bfloat16):
    result = jax.random.normal(key, extent, jnp.float32) * spread
    if len(cuts) > 0:
        result = levels(key, extent, cuts, -0.22, 0.18) * result
    return jnp.clip(result, min=-limit, max=limit).astype(kind)


def setup_inputs(seed: int = 0) -> dict:
    arg_keys = jax.random.split(jax.random.key(seed), 7)
    rhs_field = draw_rhs_field(jax.random.fold_in(arg_keys[6], 71), 0)
    neighbors = draw_neighbors(jax.random.fold_in(arg_keys[6], 71), 0)
    nu_mean = jnp.clip(jnp.exp(math.log(4.0) - 2.0794415 * jax.random.uniform(arg_keys[2], (DEG, NODES), jnp.float32) ** levels(arg_keys[2], (DEG, NODES), ((1, 16),), -0.2, 0.2)), 0.5, 4.0)
    nu_ripple = gaussian(arg_keys[3], (H, DEG, NODES), 0.04, 0.24, ((2, 16),), jnp.float32)
    mass_coeff = jnp.clip(jnp.exp(math.log(2.0) - 1.3862944 * jax.random.uniform(arg_keys[4], (NODES,), jnp.float32) ** levels(arg_keys[4], (NODES,), ((0, 16),), -0.2, 0.2)), 0.5, 2.0)
    eddy_coeff = jnp.clip(jnp.exp(math.log(2.0) - 2.0794415 * jax.random.uniform(arg_keys[5], (NODES,), jnp.float32) ** levels(arg_keys[5], (NODES,), ((0, 16),), -0.2, 0.2)), 0.25, 2.0)
    return {"rhs_field": rhs_field, "neighbors": neighbors, "nu_mean": nu_mean, "nu_ripple": nu_ripple, "mass_coeff": mass_coeff, "eddy_coeff": eddy_coeff}


def eddy_factor(harmonics):
    harm_order = (jnp.arange(harmonics) // 2 + 1).astype(jnp.float32)
    sign_vals = jnp.where(jnp.arange(harmonics) % 2 == 0, 1.0, -1.0).astype(jnp.float32)
    return 4.0 * harm_order / harmonics * sign_vals

def swap_pairs(vector_in):
    shaped = vector_in.reshape(vector_in.shape[0] // 2, 2, vector_in.shape[1])
    return shaped[:, ::-1, :].reshape(vector_in.shape)

def apply_operator(vector_in, kernel_hat, neighbors, mass_coeff, eddy_coeff, factor):
    gradients = vector_in[:, None, :] - vector_in[:, neighbors]
    fluxes = jnp.fft.irfft(kernel_hat * jnp.fft.rfft(gradients, axis=0), n=vector_in.shape[0], axis=0)
    fluxes = fluxes.astype(jnp.float32)
    return lax.optimization_barrier(jnp.sum(fluxes, axis=1)) + mass_coeff[None, :] * vector_in + eddy_coeff[None, :] * factor[:, None] * swap_pairs(vector_in)

def least_squares(columns, beta_norm):
    steps_total = len(columns)
    rot_cos, rot_sin = ([], [])
    target = [beta_norm] + [jnp.zeros((), jnp.float32)] * steps_total
    triangle = []
    for j in range(steps_total):
        column_vals = list(columns[j])
        for i in range(j):
            first, second = (column_vals[i], column_vals[i + 1])
            column_vals[i] = rot_cos[i] * first + rot_sin[i] * second
            column_vals[i + 1] = rot_cos[i] * second - rot_sin[i] * first
        radius = jnp.sqrt(column_vals[j] * column_vals[j] + column_vals[j + 1] * column_vals[j + 1])
        cosine = column_vals[j] / radius
        sine_val = column_vals[j + 1] / radius
        rot_cos.append(cosine)
        rot_sin.append(sine_val)
        column_vals[j] = radius
        target[j + 1] = -sine_val * target[j]
        target[j] = cosine * target[j]
        triangle.append(column_vals[:j + 1])
    coeffs = [None] * steps_total
    for j in reversed(range(steps_total)):
        running = target[j]
        for k in range(j + 1, steps_total):
            running = running - triangle[k][j] * coeffs[k]
        coeffs[j] = running / triangle[j][j]
    return coeffs

def reference(rhs_field, neighbors, nu_mean, nu_ripple, mass_coeff, eddy_coeff):
    harmonics = rhs_field.shape[0]
    kernel = nu_ripple.at[0].add(nu_mean)
    kernel_hat = jnp.fft.rfft(kernel, axis=0)
    factor = eddy_factor(harmonics)

    def operate(vector_in):
        return apply_operator(vector_in, kernel_hat, neighbors, mass_coeff, eddy_coeff, factor)
    beta_norm = jnp.sqrt(jnp.sum(rhs_field * rhs_field))
    krylov = [rhs_field / beta_norm]
    columns = []
    for j in range(ITERS):
        image = operate(krylov[j])
        projected = [jnp.sum(krylov[i] * image) for i in range(j + 1)]
        for i in range(j + 1):
            image = image - projected[i] * krylov[i]
        length = jnp.sqrt(jnp.sum(image * image))
        columns.append(projected + [length])
        if j + 1 < ITERS:
            krylov.append(image / length)
    coeffs = least_squares(columns, beta_norm)
    correction = coeffs[0] * krylov[0]
    for j in range(1, ITERS):
        correction = correction + coeffs[j] * krylov[j]
    residual = rhs_field - operate(correction)
    return (correction, residual)
```

```python
import functools

import jax
import jax.numpy as jnp
import ml_dtypes
import numpy as np
from jax import lax
from jax.experimental import pallas as pl
from jax.experimental.pallas import tpu as pltpu
from jax.sharding import PartitionSpec as P

IF = 64
ITERS = 8
MESH = pl.DeviceIdType.MESH


def tables(harmonics):
    half = harmonics // 2
    index = np.arange(harmonics)
    phase = 2.0 * np.pi * ((index[:, None] * index[None, :]) % harmonics) / harmonics
    plain = np.concatenate([np.cos(phase[:half]), -np.sin(phase[:half])], axis=0)
    plain[half] = np.cos(phase[half])
    scale = np.full((harmonics, 1), np.sqrt(2.0 / harmonics))
    scale[0] = scale[half] = np.sqrt(1.0 / harmonics)
    unitary = plain * scale
    swap = np.zeros((harmonics, harmonics))
    swap[index, index ^ 1] = 4.0 * (index // 2 + 1) / harmonics * np.where(index % 2 == 0, 1.0, -1.0)
    swap = unitary @ swap @ unitary.T
    high = swap.astype(np.float32).astype(ml_dtypes.bfloat16)
    low = (swap - high.astype(np.float64)).astype(ml_dtypes.bfloat16)
    swap_parts = np.concatenate([high, low, high, low], axis=1)
    return plain.astype(np.float32), unitary.astype(np.float32), unitary.T.astype(np.float32), swap_parts


def split_parts(value, count):
    parts = []
    for _ in range(count):
        part = value.astype(jnp.bfloat16)
        parts.append(part)
        value = value - part.astype(jnp.float32)
    return parts


def dot_high(left, right):
    return jnp.dot(left, right, precision=lax.Precision.HIGHEST, preferred_element_type=jnp.float32)


def solve_least_squares(columns, beta):
    steps = len(columns)
    rot_cos, rot_sin = [], []
    target = [beta] + [None] * steps
    triangle = []
    for j in range(steps):
        col = list(columns[j])
        for i in range(j):
            first, second = col[i], col[i + 1]
            col[i] = rot_cos[i] * first + rot_sin[i] * second
            col[i + 1] = rot_cos[i] * second - rot_sin[i] * first
        radius = jnp.sqrt(col[j] * col[j] + col[j + 1] * col[j + 1])
        cosine, sine = col[j] / radius, col[j + 1] / radius
        rot_cos.append(cosine)
        rot_sin.append(sine)
        col[j] = radius
        target[j + 1] = -sine * target[j]
        target[j] = cosine * target[j]
        triangle.append(col[: j + 1])
    coeffs = [None] * steps
    for j in reversed(range(steps)):
        running = target[j]
        for k in range(j + 1, steps):
            running = running - triangle[k][j] * coeffs[k]
        coeffs[j] = running / triangle[j][j]
    return coeffs


def gmres_kernel(
    n_harm, n_space,
    rhs_ref, nbr_ref, mean_ref, rip_ref, mass_ref, eddy_ref,
    plain_ref, unit_ref, unit_t_ref, swap_ref,
    corr_ref, res_ref,
    rhs_all, onehot, k_re, k_re2, k_im, basis, image, field, halo, msg, dots_in, phys, phys_in,
    rhs_send, rhs_recv, halo_send, halo_recv, dot_send, dot_recv, out_send, out_recv,
):
    block, own2 = rhs_ref.shape
    own = own2 // 2
    harmonics = rip_ref.shape[0]
    half = harmonics // 2
    degree = nbr_ref.shape[0]
    group = n_harm // 2
    places = 2 * n_space
    h = lax.axis_index("harm")
    s = lax.axis_index("space")
    lane_rank = lax.rem(h, group)

    def side_of(harm, space):
        return lax.rem(harm // group + space, 2)

    side = side_of(h, s)
    place = 2 * s + side

    def device_at(position):
        space = position // 2
        return (lax.rem(lax.rem(position, 2) + space, 2) * group + lane_rank, space)

    def lanes(which):
        return pl.ds(pl.multiple_of(which * own, own), own)

    def rows(which):
        return pl.ds(pl.multiple_of(which * block, block), block)

    barrier = pltpu.get_barrier_semaphore()

    def greet(offset, carry):
        pl.semaphore_signal(barrier, inc=1, device_id=device_at(lax.rem(place + offset, places)), device_id_type=MESH)
        return carry

    lax.fori_loop(1, places, greet, 0)
    extra = [o for o in range(1, n_harm) if o % group != 0]
    for o in extra:
        pl.semaphore_signal(barrier, inc=1, device_id=(lax.rem(h + o, n_harm), s), device_id_type=MESH)
    pl.semaphore_wait(barrier, places - 1 + len(extra))

    rhs_copies = []
    for o in range(1, n_harm):
        peer = lax.rem(h + o, n_harm)
        copy = pltpu.make_async_remote_copy(
            src_ref=rhs_ref.at[:, lanes(side_of(peer, s))],
            dst_ref=rhs_all.at[rows(h)],
            send_sem=rhs_send.at[o - 1],
            recv_sem=rhs_recv.at[o - 1],
            device_id=(peer, s),
            device_id_type=MESH,
        )
        copy.start()
        rhs_copies.append(copy)
    rhs_all[rows(h)] = rhs_ref[:, lanes(side)]

    first_row = lax.broadcasted_iota(jnp.int32, (half, own), 0) == 0
    row_index = lax.broadcasted_iota(jnp.int32, (own2, own), 0)
    start = place * own
    for d in range(degree):
        spectrum = dot_high(plain_ref[...], rip_ref[:, d, lanes(side)])
        mean = mean_ref[d : d + 1, lanes(side)]
        real, imag = spectrum[:half], spectrum[half:]
        k_re[d] = real + mean
        k_re2[d] = jnp.where(first_row, imag, real) + mean
        k_im[d] = jnp.where(first_row, 0.0, imag)
        spot = jnp.bitwise_and(nbr_ref[d : d + 1, lanes(side)] - start, own2 - 1)
        onehot[:, d * own : (d + 1) * own] = jnp.where(row_index == spot, 1.0, 0.0).astype(jnp.bfloat16)
    mass = mass_ref[:, lanes(side)]
    eddy = eddy_ref[:, lanes(side)]
    for copy in rhs_copies:
        copy.wait_recv()

    lane_index = lax.broadcasted_iota(jnp.int32, (1, 128), 1)
    near = lax.broadcasted_iota(jnp.int32, (harmonics, own), 1) < IF
    left = device_at(lax.rem(place + places - 1, places))
    right = device_at(lax.rem(place + 1, places))
    halo_copies = []

    def send_halo(k, source):
        for way, target in ((0, right), (1, left)):
            copy = pltpu.make_async_remote_copy(
                src_ref=source,
                dst_ref=halo.at[k, way],
                send_sem=halo_send.at[k, way],
                recv_sem=halo_recv.at[k, way],
                device_id=target,
                device_id_type=MESH,
            )
            copy.start()
            halo_copies.append(copy)

    def operate(k, vector):
        mine = split_parts(vector, 3)
        swapped = jnp.dot(
            swap_ref[...], jnp.concatenate([mine[0], mine[0], mine[1], mine[1]], axis=0),
            preferred_element_type=jnp.float32,
        )
        total = mass * vector + eddy * swapped
        halo_copies[2 * k].wait_recv()
        halo_copies[2 * k + 1].wait_recv()
        outer = split_parts(jnp.where(near, halo[k, 1], halo[k, 0]), 3)
        stacked = jnp.concatenate(
            [jnp.concatenate([a, b], axis=1) for a, b in zip(mine, outer)], axis=0
        )
        v_re, v_im = vector[:half], vector[half:]
        sum_re, sum_im = total[:half], total[half:]
        for d in range(0, degree, 2):
            far = jnp.dot(stacked, onehot[:, d * own : (d + 2) * own], preferred_element_type=jnp.float32)
            far = far[:harmonics] + far[harmonics : 2 * harmonics] + far[2 * harmonics :]
            for e in range(2):
                g_re = v_re - far[:half, e * own : (e + 1) * own]
                g_im = v_im - far[half:, e * own : (e + 1) * own]
                sum_re += k_re[d + e] * g_re - k_im[d + e] * g_im
                sum_im += k_re2[d + e] * g_im + k_im[d + e] * g_re
        return jnp.concatenate([sum_re, sum_im], axis=0)

    def total_of(product):
        return jnp.sum(jnp.sum(product, axis=0, keepdims=True), axis=1, keepdims=True)

    def send_dots(k, products):
        row = jnp.zeros((1, 128), jnp.float32)
        for i, product in enumerate(products):
            row = jnp.where(lane_index == i, total_of(product), row)
        msg[k] = row

        def send(offset, carry):
            pltpu.make_async_remote_copy(
                src_ref=msg.at[k],
                dst_ref=dots_in.at[k, offset - 1],
                send_sem=dot_send.at[k],
                recv_sem=dot_recv.at[k],
                device_id=device_at(lax.rem(place + offset, places)),
                device_id_type=MESH,
            ).start()
            return carry

        lax.fori_loop(1, places, send, 0)

    def wait_dots(sem, k):
        pltpu.make_async_copy(dots_in.at[k], dots_in.at[k], sem.at[k]).wait()

    def receive_dots(k, count):
        wait_dots(dot_recv, k)
        row = msg[k] + jnp.sum(dots_in[k], axis=0)
        return [row[:, i : i + 1] for i in range(count)]

    field[0] = dot_high(unit_ref[...], rhs_all[...])
    send_halo(0, field.at[0])
    rhs = field[0]
    rhs_image = operate(0, rhs)
    field[1] = rhs_image
    send_halo(1, field.at[1])
    send_dots(0, [rhs * rhs, rhs * rhs_image, rhs_image * rhs_image])
    second = operate(1, rhs_image)
    rr, ru, uu = receive_dots(0, 3)
    beta = jnp.sqrt(rr)
    theta = ru / rr
    inverse = 1.0 / beta
    length = jnp.sqrt((uu - ru * theta) / rr)
    basis[0] = rhs * inverse
    image[0] = (rhs_image - theta * rhs) * inverse
    shifted = (second - theta * rhs_image) * inverse - theta * image[0]
    columns = [[theta, length]]
    basis[1] = image[0] / length
    image[1] = shifted / length
    for j in range(1, ITERS):
        current = image[j]
        if j + 1 < ITERS:
            send_halo(j + 1, image.at[j])
        send_dots(j, [basis[i] * current for i in range(j + 1)] + [current * current])
        if j + 1 < ITERS:
            following = operate(j + 1, current) - theta * current
        found = receive_dots(j, j + 2)
        dots, squared = found[: j + 1], found[j + 1]
        for value in dots:
            squared = squared - value * value
        length = jnp.sqrt(squared)
        columns.append(dots[:j] + [dots[j] + theta, length])
        if j + 1 < ITERS:
            scale = 1.0 / length
            for i, value in enumerate(dots):
                current = current - value * basis[i]
                following = following - value * image[i]
            basis[j + 1] = current * scale
            image[j + 1] = following * scale
    coeffs = solve_least_squares(columns, beta)
    correction = coeffs[0] * basis[0]
    product = coeffs[0] * image[0]
    for j in range(1, ITERS):
        correction = correction + coeffs[j] * basis[j]
        product = product + coeffs[j] * image[j]
    residual = rhs - product - theta * correction
    phys[0] = dot_high(unit_t_ref[...], correction)
    phys[1] = dot_high(unit_t_ref[...], residual)

    other = lax.rem(h + group, n_harm)
    final = pltpu.make_async_remote_copy(
        src_ref=phys.at[:, rows(other)],
        dst_ref=phys_in,
        send_sem=out_send,
        recv_sem=out_recv,
        device_id=(other, s),
        device_id_type=MESH,
    )
    final.start()
    corr_ref[:, lanes(side)] = phys[0, rows(h)]
    res_ref[:, lanes(side)] = phys[1, rows(h)]
    for copy in rhs_copies + halo_copies:
        copy.wait_send()
    for k in range(ITERS):
        wait_dots(dot_send, k)
    final.wait()
    corr_ref[:, lanes(1 - side)] = phys_in[0]
    res_ref[:, lanes(1 - side)] = phys_in[1]


def per_device(n_harm, n_space, rhs_field, neighbors, nu_mean, nu_ripple, mass_coeff, eddy_coeff):
    block, own2 = rhs_field.shape
    own = own2 // 2
    harmonics, degree = nu_ripple.shape[:2]
    plain, unit, unit_t, swap_parts = tables(harmonics)
    places = 2 * n_space
    f32 = jnp.float32
    vmem = pl.BlockSpec(memory_space=pltpu.VMEM)
    dma = pltpu.SemaphoreType.DMA
    return pl.pallas_call(
        functools.partial(gmres_kernel, n_harm, n_space),
        out_shape=(jax.ShapeDtypeStruct((block, own2), f32),) * 2,
        in_specs=[vmem] * 10,
        out_specs=(vmem, vmem),
        scratch_shapes=[
            pltpu.VMEM((harmonics, own), f32),
            pltpu.VMEM((own2, degree * own), jnp.bfloat16),
            pltpu.VMEM((degree, harmonics // 2, own), f32),
            pltpu.VMEM((degree, harmonics // 2, own), f32),
            pltpu.VMEM((degree, harmonics // 2, own), f32),
            pltpu.VMEM((ITERS, harmonics, own), f32),
            pltpu.VMEM((ITERS, harmonics, own), f32),
            pltpu.VMEM((2, harmonics, own), f32),
            pltpu.VMEM((ITERS, 2, harmonics, own), f32),
            pltpu.VMEM((ITERS, 1, 128), f32),
            pltpu.VMEM((ITERS, places - 1, 1, 128), f32),
            pltpu.VMEM((2, harmonics, own), f32),
            pltpu.VMEM((2, block, own), f32),
            dma((n_harm - 1,)),
            dma((n_harm - 1,)),
            dma((ITERS, 2)),
            dma((ITERS, 2)),
            dma((ITERS,)),
            dma((ITERS,)),
            dma,
            dma,
        ],
        compiler_params=pltpu.CompilerParams(
            collective_id=0, has_side_effects=True, vmem_limit_bytes=32 * 1024 * 1024
        ),
    )(
        rhs_field, neighbors, nu_mean, nu_ripple,
        mass_coeff.reshape(1, own2), eddy_coeff.reshape(1, own2),
        jnp.asarray(plain), jnp.asarray(unit), jnp.asarray(unit_t), jnp.asarray(swap_parts),
    )


def solution(mesh):
    return jax.shard_map(
        functools.partial(per_device, mesh.shape["harm"], mesh.shape["space"]),
        mesh=mesh,
        in_specs=(
            P("harm", "space"),
            P(None, "space"),
            P(None, "space"),
            P(None, None, "space"),
            P("space"),
            P("space"),
        ),
        out_specs=(P("harm", "space"), P("harm", "space")),
        check_vma=False,
    )
```

```python
import functools

import jax
import jax.numpy as jnp
import ml_dtypes
import numpy as np
from jax import lax
from jax.experimental import pallas as pl
from jax.experimental.pallas import tpu as pltpu
from jax.sharding import PartitionSpec as P

IF = 64
ITERS = 8
MESH = pl.DeviceIdType.MESH


def tables(harmonics):
    half = harmonics // 2
    index = np.arange(harmonics)
    phase = 2.0 * np.pi * ((index[:, None] * index[None, :]) % harmonics) / harmonics
    plain = np.concatenate([np.cos(phase[:half]), -np.sin(phase[:half])], axis=0)
    plain[half] = np.cos(phase[half])
    scale = np.full((harmonics, 1), np.sqrt(2.0 / harmonics))
    scale[0] = scale[half] = np.sqrt(1.0 / harmonics)
    unitary = plain * scale
    swap = np.zeros((harmonics, harmonics))
    swap[index, index ^ 1] = 4.0 * (index // 2 + 1) / harmonics * np.where(index % 2 == 0, 1.0, -1.0)
    swap = unitary @ swap @ unitary.T
    high = swap.astype(np.float32).astype(ml_dtypes.bfloat16)
    low = (swap - high.astype(np.float64)).astype(ml_dtypes.bfloat16)
    swap_parts = np.concatenate([high, low, high, low], axis=1)
    return plain.astype(np.float32), unitary.astype(np.float32), unitary.T.astype(np.float32), swap_parts


def split_parts(value, count):
    parts = []
    for _ in range(count):
        part = value.astype(jnp.bfloat16)
        parts.append(part)
        value = value - part.astype(jnp.float32)
    return parts


def dot_high(left, right):
    return jnp.dot(left, right, precision=lax.Precision.HIGHEST, preferred_element_type=jnp.float32)


class LeastSquares:
    def __init__(self, beta):
        self.rotations = []
        self.triangle = []
        self.target = [beta]

    def add(self, column):
        col = list(column)
        for i, (cosine, sine) in enumerate(self.rotations):
            first, second = col[i], col[i + 1]
            col[i] = cosine * first + sine * second
            col[i + 1] = cosine * second - sine * first
        j = len(self.rotations)
        radius = jnp.sqrt(col[j] * col[j] + col[j + 1] * col[j + 1])
        cosine, sine = col[j] / radius, col[j + 1] / radius
        self.rotations.append((cosine, sine))
        col[j] = radius
        self.target.append(-sine * self.target[j])
        self.target[j] = cosine * self.target[j]
        self.triangle.append(col[: j + 1])

    def solve(self):
        steps = len(self.triangle)
        coeffs = [None] * steps
        for j in reversed(range(steps)):
            running = self.target[j]
            for k in range(j + 1, steps):
                running = running - self.triangle[k][j] * coeffs[k]
            coeffs[j] = running / self.triangle[j][j]
        return coeffs


def gmres_kernel(
    n_harm, n_space,
    rhs_ref, nbr_hbm, mean_hbm, rip_hbm, mass_hbm, eddy_hbm,
    plain_hbm, unit_hbm, unit_t_hbm, swap_hbm,
    corr_ref, res_ref,
    nbr_ref, mean_ref, rip_ref, mass_ref, eddy_ref, plain_ref, unit_ref, unit_t_ref, swap_ref, load_sem,
    cross_send, cross_recv,
    rhs_all, hot_own, hot_ghost, k_re, k_re2, k_im, basis, image, image2, field, halo, msg, dots_in, phys, phys_in,
    rhs_send, rhs_recv, halo_send, halo_recv, dot_send, dot_recv, out_send, out_recv,
):
    block, own2 = rhs_ref.shape
    own = own2 // 2
    harmonics = rip_hbm.shape[0]
    half = harmonics // 2
    degree = nbr_hbm.shape[0]
    group = n_harm // 2
    places = 2 * n_space
    h = lax.axis_index("harm")
    s = lax.axis_index("space")
    lane_rank = lax.rem(h, group)

    def side_of(harm, space):
        return lax.rem(harm // group + space, 2)

    side = side_of(h, s)
    place = 2 * s + side

    def device_at(position):
        space = position // 2
        return (lax.rem(lax.rem(position, 2) + space, 2) * group + lane_rank, space)

    def lanes(which):
        return pl.ds(pl.multiple_of(which * own, own), own)

    def rows(which):
        return pl.ds(pl.multiple_of(which * block, block), block)

    edge_data = (
        (nbr_hbm, nbr_ref), (mean_hbm, mean_ref), (mass_hbm, mass_ref), (rip_hbm, rip_ref), (eddy_hbm, eddy_ref)
    )
    loads = []

    def load(source, target):
        copy = pltpu.make_async_copy(source, target, load_sem.at[len(loads)])
        copy.start()
        loads.append(copy)

    def part(source, which):
        return source.at[:, :, lanes(which)] if len(source.shape) == 3 else source.at[:, lanes(which)]

    for source, target in edge_data:
        load(part(source, side), target.at[0])
    load(plain_hbm, plain_ref)
    load(rhs_ref.at[:, lanes(side)], rhs_all.at[rows(h)])
    load(unit_hbm, unit_ref)
    load(swap_hbm, swap_ref)
    load(unit_t_hbm, unit_t_ref)
    for source, target in edge_data:
        load(part(source, 1 - side), target.at[1])

    barrier = pltpu.get_barrier_semaphore()

    def greet(offset, carry):
        pl.semaphore_signal(barrier, inc=1, device_id=device_at(lax.rem(place + offset, places)), device_id_type=MESH)
        return carry

    lax.fori_loop(1, places, greet, 0)
    extra = [o for o in range(1, n_harm) if o % group != 0]
    for o in extra:
        pl.semaphore_signal(barrier, inc=1, device_id=(lax.rem(h + o, n_harm), s), device_id_type=MESH)
    pl.semaphore_wait(barrier, places - 1 + len(extra))

    rhs_copies = []
    for o in range(1, n_harm):
        peer = lax.rem(h + o, n_harm)
        copy = pltpu.make_async_remote_copy(
            src_ref=rhs_ref.at[:, lanes(side_of(peer, s))],
            dst_ref=rhs_all.at[rows(h)],
            send_sem=rhs_send.at[o - 1],
            recv_sem=rhs_recv.at[o - 1],
            device_id=(peer, s),
            device_id_type=MESH,
        )
        copy.start()
        rhs_copies.append(copy)
    cross = device_at(lax.rem(place + places + 2 * side - 1, places))
    cross_copies = []
    for i, (source, target) in enumerate(edge_data):
        copy = pltpu.make_async_remote_copy(
            src_ref=part(source, side),
            dst_ref=target.at[2],
            send_sem=cross_send.at[i],
            recv_sem=cross_recv.at[i],
            device_id=cross,
            device_id_type=MESH,
        )
        copy.start()
        cross_copies.append(copy)

    lane_index = lax.broadcasted_iota(jnp.int32, (1, 128), 1)
    near = lax.broadcasted_iota(jnp.int32, (harmonics, own), 1) < IF
    left = device_at(lax.rem(place + places - 1, places))
    right = device_at(lax.rem(place + 1, places))
    halo_copies = []

    def send_halo(k, source):
        for way, target in ((0, right), (1, left)):
            copy = pltpu.make_async_remote_copy(
                src_ref=source,
                dst_ref=halo.at[k, way],
                send_sem=halo_send.at[k, way],
                recv_sem=halo_recv.at[k, way],
                device_id=target,
                device_id_type=MESH,
            )
            copy.start()
            halo_copies.append(copy)

    def total_of(product):
        return jnp.sum(jnp.sum(product, axis=0, keepdims=True), axis=1, keepdims=True)

    def send_dots(k, products):
        row = jnp.zeros((1, 128), jnp.float32)
        for i, product in enumerate(products):
            row = jnp.where(lane_index == i, total_of(product), row)
        msg[k] = row

        def send(offset, carry):
            pltpu.make_async_remote_copy(
                src_ref=msg.at[k],
                dst_ref=dots_in.at[k, offset - 1],
                send_sem=dot_send.at[k],
                recv_sem=dot_recv.at[k],
                device_id=device_at(lax.rem(place + offset, places)),
                device_id_type=MESH,
            ).start()
            return carry

        lax.fori_loop(1, places, send, 0)

    def wait_dots(sem, k):
        pltpu.make_async_copy(dots_in.at[k], dots_in.at[k], sem.at[k]).wait()

    def receive_dots(k, count):
        wait_dots(dot_recv, k)
        row = msg[k] + jnp.sum(dots_in[k], axis=0)
        return [row[:, i : i + 1] for i in range(count)]

    for copy in loads:
        copy.wait()
    start = place * own
    total_nodes = own * places
    diagonal = mass_ref[0]
    here = start + lax.broadcasted_iota(jnp.int32, (1, own), 1)
    for d in range(degree):
        used = nbr_ref[0, d : d + 1, :] != here
        diagonal = diagonal + jnp.where(used, mean_ref[0, d : d + 1, :], 0.0)
    last = ITERS // 2
    send_dots(last, [diagonal])

    first_row = lax.broadcasted_iota(jnp.int32, (half, own), 0) == 0

    def prepare(where_to, ripple, mean, spot, hot):
        height = hot.shape[0]
        row_index = lax.broadcasted_iota(jnp.int32, (height, own), 0)
        for d in range(degree):
            spectrum = dot_high(plain_ref[...], ripple(d))
            real, imag = spectrum[:half], spectrum[half:]
            k_re[where_to, d] = real + mean(d)
            k_re2[where_to, d] = jnp.where(first_row, imag, real) + mean(d)
            k_im[where_to, d] = jnp.where(first_row, 0.0, imag)
            hot[:, d * own : (d + 1) * own] = jnp.where(row_index == spot(d), 1.0, 0.0).astype(jnp.bfloat16)

    for copy in rhs_copies:
        copy.wait_recv()
    field[0] = dot_high(unit_ref[...], rhs_all[...])
    send_halo(0, field.at[0])
    prepare(
        0,
        lambda d: rip_ref[0, :, d, :],
        lambda d: mean_ref[0, d : d + 1, :],
        lambda d: jnp.bitwise_and(nbr_ref[0, d : d + 1, :] - start, own2 - 1),
        hot_own,
    )
    for copy in cross_copies:
        copy.wait_recv()
    lane_full = lax.broadcasted_iota(jnp.int32, (harmonics, own), 1)
    from_partner = jnp.where(lane_full < IF, 0, 1) == side

    def ghost(ref, index):
        partner, outer = ref[(1, *index)], ref[(2, *index)]
        return jnp.where(from_partner[: partner.shape[0]], partner, outer)

    def ghost_spot(d):
        place_of = ghost(nbr_ref, (slice(d, d + 1), slice(None))) - start
        place_of = jnp.where(place_of < 0, place_of + total_nodes, place_of)
        return jnp.where(place_of >= total_nodes - own, place_of - (total_nodes - 3 * own), place_of)

    prepare(
        1,
        lambda d: ghost(rip_ref, (slice(None), d, slice(None))),
        lambda d: ghost(mean_ref, (slice(d, d + 1), slice(None))),
        ghost_spot,
        hot_ghost,
    )
    whole_row = (slice(None), slice(None))
    wait_dots(dot_recv, last)
    theta = jnp.sum(msg[last] + jnp.sum(dots_in[last], axis=0), axis=1, keepdims=True) / total_nodes
    mass = [mass_ref[0] - theta, ghost(mass_ref, whole_row) - theta]
    eddy = [eddy_ref[0], ghost(eddy_ref, whole_row)]

    def stack(*tiles):
        pieces = [split_parts(tile, 3) for tile in tiles]
        return jnp.concatenate([jnp.concatenate(row, axis=1) for row in zip(*pieces)], axis=0)

    def operate(which, vector, stacked, hot):
        high, low = split_parts(vector, 2)
        swapped = jnp.dot(
            swap_ref[...], jnp.concatenate([high, high, low, low], axis=0),
            preferred_element_type=jnp.float32,
        )
        total = mass[which] * vector + eddy[which] * swapped
        v_re, v_im = vector[:half], vector[half:]
        sum_re, sum_im = total[:half], total[half:]
        for d in range(0, degree, 2):
            far = jnp.dot(stacked, hot[:, d * own : (d + 2) * own], preferred_element_type=jnp.float32)
            far = far[:harmonics] + far[harmonics : 2 * harmonics] + far[2 * harmonics :]
            for e in range(2):
                g_re = v_re - far[:half, e * own : (e + 1) * own]
                g_im = v_im - far[half:, e * own : (e + 1) * own]
                re, re2, im = k_re[which, d + e], k_re2[which, d + e], k_im[which, d + e]
                sum_re += re * g_re - im * g_im
                sum_im += re2 * g_im + im * g_re
        return jnp.concatenate([sum_re, sum_im], axis=0)

    def operate_twice(k, vector):
        halo_copies[2 * k].wait_recv()
        halo_copies[2 * k + 1].wait_recv()
        before, after = halo[k, 0], halo[k, 1]
        outer = jnp.where(near, after, before)
        once = operate(0, vector, stack(vector, outer), hot_own)
        once_outer = operate(1, outer, stack(vector, after, before), hot_ghost)
        return once, operate(0, once, stack(once, once_outer), hot_own)

    rhs = field[0]
    first, second = operate_twice(0, rhs)
    field[1] = second
    send_halo(1, field.at[1])
    send_dots(0, [rhs * rhs, rhs * first, rhs * second, first * first, first * second, second * second])
    third, fourth = operate_twice(1, second)
    rr, *found = receive_dots(0, 6)
    per_rr = 1.0 / rr
    beta = jnp.sqrt(rr)
    inverse = 1.0 / beta
    basis[0] = rhs * inverse
    image[0] = first * inverse
    image2[0] = second * inverse
    third, fourth = third * inverse, fourth * inverse
    found = [value * per_rr for value in found]
    fit = LeastSquares(beta)
    shifted = []
    pending = []

    def flush():
        for column in pending:
            i = len(fit.triangle)
            fit.add(column[:i] + [column[i] + theta] + column[i + 1 :])
        pending.clear()

    for m in range(0, ITERS, 2):
        on_more = m + 2 < ITERS
        x1, x2 = image[m], image2[m]
        if m > 0:
            if on_more:
                send_halo(m // 2 + 1, image2.at[m])
            kept = [basis[i] for i in range(m + 1)]
            send_dots(
                m // 2,
                [v * x1 for v in kept] + [v * x2 for v in kept] + [x1 * x1, x1 * x2, x2 * x2],
            )
            if on_more:
                third, fourth = operate_twice(m // 2 + 1, x2)
            flush()
            found = receive_dots(m // 2, 2 * m + 5)
        dot1, dot2 = found[: m + 1], found[m + 1 : 2 * m + 2]
        s11, s12, s22 = found[2 * m + 2 :]
        for p, q in zip(dot1, dot2):
            s11, s12, s22 = s11 - p * p, s12 - p * q, s22 - q * q
        length1 = jnp.sqrt(s11)
        scale1 = 1.0 / length1
        dot2.append(s12 * scale1)
        length2 = jnp.sqrt(s22 - dot2[-1] * dot2[-1])
        scale2 = 1.0 / length2
        column = dot1 + [length1]
        shifted.append(column)
        pending.append(column)
        column = dot2 + [length2]
        for i, value in enumerate(dot1):
            for k, entry in enumerate(shifted[i]):
                column[k] = column[k] - value * entry
        column = [entry * scale1 for entry in column]
        shifted.append(column)
        pending.append(column)
        new_v, new_p = x1, x2
        for i, value in enumerate(dot1):
            new_v = new_v - value * basis[i]
            new_p = new_p - value * image[i]
        basis[m + 1] = new_v * scale1
        image[m + 1] = new_p * scale1
        if on_more:
            new_q = third
            for i, value in enumerate(dot1):
                new_q = new_q - value * image2[i]
            image2[m + 1] = new_q * scale1
            new_v, new_p, new_q = x2, third, fourth
            for i, value in enumerate(dot2):
                new_v = new_v - value * basis[i]
                new_p = new_p - value * image[i]
                new_q = new_q - value * image2[i]
            basis[m + 2] = new_v * scale2
            image[m + 2] = new_p * scale2
            image2[m + 2] = new_q * scale2
    flush()
    coeffs = fit.solve()
    correction = coeffs[0] * basis[0]
    product = coeffs[0] * image[0]
    for j in range(1, ITERS):
        correction = correction + coeffs[j] * basis[j]
        product = product + coeffs[j] * image[j]
    residual = rhs - product - theta * correction
    phys[0] = dot_high(unit_t_ref[...], correction)
    phys[1] = dot_high(unit_t_ref[...], residual)

    other = lax.rem(h + group, n_harm)
    final = pltpu.make_async_remote_copy(
        src_ref=phys.at[:, rows(other)],
        dst_ref=phys_in,
        send_sem=out_send,
        recv_sem=out_recv,
        device_id=(other, s),
        device_id_type=MESH,
    )
    final.start()
    corr_ref[:, lanes(side)] = phys[0, rows(h)]
    res_ref[:, lanes(side)] = phys[1, rows(h)]
    for copy in rhs_copies + cross_copies + halo_copies:
        copy.wait_send()
    for k in range(ITERS // 2 + 1):
        wait_dots(dot_send, k)
    final.wait()
    corr_ref[:, lanes(1 - side)] = phys_in[0]
    res_ref[:, lanes(1 - side)] = phys_in[1]


def per_device(n_harm, n_space, rhs_field, neighbors, nu_mean, nu_ripple, mass_coeff, eddy_coeff):
    block, own2 = rhs_field.shape
    own = own2 // 2
    harmonics, degree = nu_ripple.shape[:2]
    plain, unit, unit_t, swap_parts = tables(harmonics)
    places = 2 * n_space
    f32 = jnp.float32
    vmem = pl.BlockSpec(memory_space=pltpu.VMEM)
    dma = pltpu.SemaphoreType.DMA
    return pl.pallas_call(
        functools.partial(gmres_kernel, n_harm, n_space),
        out_shape=(jax.ShapeDtypeStruct((block, own2), f32),) * 2,
        in_specs=[pl.BlockSpec(memory_space=pltpu.HBM)] * 10,
        out_specs=(vmem, vmem),
        scratch_shapes=[
            pltpu.VMEM((3, degree, own), neighbors.dtype),
            pltpu.VMEM((3, degree, own), f32),
            pltpu.VMEM((3, harmonics, degree, own), f32),
            pltpu.VMEM((3, 1, own), f32),
            pltpu.VMEM((3, 1, own), f32),
            pltpu.VMEM((harmonics, harmonics), f32),
            pltpu.VMEM((harmonics, harmonics), f32),
            pltpu.VMEM((harmonics, harmonics), f32),
            pltpu.VMEM(swap_parts.shape, jnp.bfloat16),
            dma((15,)),
            dma((5,)),
            dma((5,)),
            pltpu.VMEM((harmonics, own), f32),
            pltpu.VMEM((own2, degree * own), jnp.bfloat16),
            pltpu.VMEM((3 * own, degree * own), jnp.bfloat16),
            pltpu.VMEM((2, degree, harmonics // 2, own), f32),
            pltpu.VMEM((2, degree, harmonics // 2, own), f32),
            pltpu.VMEM((2, degree, harmonics // 2, own), f32),
            pltpu.VMEM((ITERS, harmonics, own), f32),
            pltpu.VMEM((ITERS, harmonics, own), f32),
            pltpu.VMEM((ITERS, harmonics, own), f32),
            pltpu.VMEM((2, harmonics, own), f32),
            pltpu.VMEM((ITERS // 2, 2, harmonics, own), f32),
            pltpu.VMEM((ITERS // 2 + 1, 1, 128), f32),
            pltpu.VMEM((ITERS // 2 + 1, places - 1, 1, 128), f32),
            pltpu.VMEM((2, harmonics, own), f32),
            pltpu.VMEM((2, block, own), f32),
            dma((n_harm - 1,)),
            dma((n_harm - 1,)),
            dma((ITERS // 2, 2)),
            dma((ITERS // 2, 2)),
            dma((ITERS // 2 + 1,)),
            dma((ITERS // 2 + 1,)),
            dma,
            dma,
        ],
        compiler_params=pltpu.CompilerParams(
            collective_id=0, has_side_effects=True, vmem_limit_bytes=60 * 1024 * 1024
        ),
    )(
        rhs_field, neighbors, nu_mean, nu_ripple,
        mass_coeff.reshape(1, own2), eddy_coeff.reshape(1, own2),
        jnp.asarray(plain), jnp.asarray(unit), jnp.asarray(unit_t), jnp.asarray(swap_parts),
    )


def solution(mesh):
    return jax.shard_map(
        functools.partial(per_device, mesh.shape["harm"], mesh.shape["space"]),
        mesh=mesh,
        in_specs=(
            P("harm", "space"),
            P(None, "space"),
            P(None, "space"),
            P(None, None, "space"),
            P("space"),
            P("space"),
        ),
        out_specs=(P("harm", "space"), P("harm", "space")),
        check_vma=False,
    )
```

```python
import functools

import jax
import jax.numpy as jnp
import ml_dtypes
import numpy as np
from jax import lax
from jax.experimental import pallas as pl
from jax.experimental.pallas import tpu as pltpu
from jax.sharding import PartitionSpec as P

IF = 64
ITERS = 8
MESH = pl.DeviceIdType.MESH


def tables(harmonics):
    half = harmonics // 2
    index = np.arange(harmonics)
    phase = 2.0 * np.pi * ((index[:, None] * index[None, :]) % harmonics) / harmonics
    plain = np.concatenate([np.cos(phase[:half]), -np.sin(phase[:half])], axis=0)
    plain[half] = np.cos(phase[half])
    scale = np.full((harmonics, 1), np.sqrt(2.0 / harmonics))
    scale[0] = scale[half] = np.sqrt(1.0 / harmonics)
    unitary = plain * scale
    swap = np.zeros((harmonics, harmonics))
    swap[index, index ^ 1] = 4.0 * (index // 2 + 1) / harmonics * np.where(index % 2 == 0, 1.0, -1.0)
    swap = unitary @ swap @ unitary.T
    high = swap.astype(np.float32).astype(ml_dtypes.bfloat16)
    low = (swap - high.astype(np.float64)).astype(ml_dtypes.bfloat16)
    swap_parts = np.concatenate([high, low, high, low], axis=1)
    return plain.astype(np.float32), unitary.astype(np.float32), unitary.T.astype(np.float32), swap_parts


def split_parts(value, count):
    parts = []
    for _ in range(count):
        part = value.astype(jnp.bfloat16)
        parts.append(part)
        value = value - part.astype(jnp.float32)
    return parts


def dot_high(left, right):
    return jnp.dot(left, right, precision=lax.Precision.HIGHEST, preferred_element_type=jnp.float32)


class LeastSquares:
    def __init__(self, beta):
        self.rotations = []
        self.triangle = []
        self.target = [beta]

    def add(self, column):
        col = list(column)
        for i, (cosine, sine) in enumerate(self.rotations):
            first, second = col[i], col[i + 1]
            col[i] = cosine * first + sine * second
            col[i + 1] = cosine * second - sine * first
        j = len(self.rotations)
        radius = jnp.sqrt(col[j] * col[j] + col[j + 1] * col[j + 1])
        cosine, sine = col[j] / radius, col[j + 1] / radius
        self.rotations.append((cosine, sine))
        col[j] = radius
        self.target.append(-sine * self.target[j])
        self.target[j] = cosine * self.target[j]
        self.triangle.append(col[: j + 1])

    def solve(self):
        steps = len(self.triangle)
        coeffs = [None] * steps
        for j in reversed(range(steps)):
            running = self.target[j]
            for k in range(j + 1, steps):
                running = running - self.triangle[k][j] * coeffs[k]
            coeffs[j] = running / self.triangle[j][j]
        return coeffs


def gmres_kernel(
    n_harm, n_space,
    rhs_ref, nbr_hbm, mean_hbm, rip_hbm, mass_hbm, eddy_hbm,
    plain_hbm, unit_hbm, unit_t_hbm, swap_hbm,
    corr_ref, res_ref,
    nbr_ref, mean_ref, rip_ref, mass_ref, eddy_ref, plain_ref, unit_ref, unit_t_ref, swap_ref, load_sem,
    packed, cross_send, cross_recv,
    rhs_all, hot_own, hot_ghost, k_re, k_re2, k_im, basis, image, image2, field, halo, msg, dots_in, phys, phys_in,
    rhs_send, rhs_recv, halo_send, halo_recv, dot_send, dot_recv, out_send, out_recv,
):
    block, own2 = rhs_ref.shape
    own = own2 // 2
    harmonics = rip_hbm.shape[0]
    half = harmonics // 2
    degree = nbr_hbm.shape[0]
    group = n_harm // 2
    places = 2 * n_space
    h = lax.axis_index("harm")
    s = lax.axis_index("space")
    lane_rank = lax.rem(h, group)

    def side_of(harm, space):
        return lax.rem(harm // group + space, 2)

    side = side_of(h, s)
    place = 2 * s + side

    def device_at(position):
        space = lax.shift_right_logical(position, 1)
        return (jnp.bitwise_and(position + space, 1) * group + lane_rank, space)

    def around(offset):
        position = place + offset
        return device_at(jnp.where(position >= places, position - places, position))

    def lanes(which):
        return pl.ds(pl.multiple_of(which * own, own), own)

    def rows(which):
        return pl.ds(pl.multiple_of(which * block, block), block)

    edge_data = (
        (nbr_hbm, nbr_ref), (mean_hbm, mean_ref), (mass_hbm, mass_ref), (rip_hbm, rip_ref), (eddy_hbm, eddy_ref)
    )
    loads = []

    def load(source, target):
        copy = pltpu.make_async_copy(source, target, load_sem.at[len(loads)])
        copy.start()
        loads.append(copy)

    def part(source, which):
        return source.at[:, :, lanes(which)] if len(source.shape) == 3 else source.at[:, lanes(which)]

    for source, target in edge_data:
        load(part(source, side), target.at[0])
    load(plain_hbm, plain_ref)
    load(rhs_ref.at[:, lanes(side)], rhs_all.at[rows(h)])
    load(unit_hbm, unit_ref)
    load(swap_hbm, swap_ref)
    load(unit_t_hbm, unit_t_ref)
    for source, target in edge_data:
        load(part(source, 1 - side), target.at[1])

    barrier = pltpu.get_barrier_semaphore()

    def greet(offset, carry):
        pl.semaphore_signal(barrier, inc=1, device_id=around(offset), device_id_type=MESH)
        return carry

    lax.fori_loop(1, places, greet, 0)
    extra = [o for o in range(1, n_harm) if o % group != 0]
    for o in extra:
        pl.semaphore_signal(barrier, inc=1, device_id=(lax.rem(h + o, n_harm), s), device_id_type=MESH)

    lane_index = lax.broadcasted_iota(jnp.int32, (1, 128), 1)
    near = lax.broadcasted_iota(jnp.int32, (harmonics, own), 1) < IF
    left = device_at(lax.rem(place + places - 1, places))
    right = device_at(lax.rem(place + 1, places))
    halo_copies = []

    def send_halo(k, source):
        for way, target in ((0, right), (1, left)):
            copy = pltpu.make_async_remote_copy(
                src_ref=source,
                dst_ref=halo.at[k, way],
                send_sem=halo_send.at[k, way],
                recv_sem=halo_recv.at[k, way],
                device_id=target,
                device_id_type=MESH,
            )
            copy.start()
            halo_copies.append(copy)

    def total_of(product):
        return jnp.sum(jnp.sum(product, axis=0, keepdims=True), axis=1, keepdims=True)

    def send_dots(k, products):
        row = jnp.zeros((1, 128), jnp.float32)
        for i, product in enumerate(products):
            row = jnp.where(lane_index == i, total_of(product), row)
        msg[k] = row

        def send(offset, carry):
            pltpu.make_async_remote_copy(
                src_ref=msg.at[k],
                dst_ref=dots_in.at[k, offset - 1],
                send_sem=dot_send.at[k],
                recv_sem=dot_recv.at[k],
                device_id=around(offset),
                device_id_type=MESH,
            ).start()
            return carry

        lax.fori_loop(1, places, send, 0)

    def wait_dots(sem, k):
        pltpu.make_async_copy(dots_in.at[k], dots_in.at[k], sem.at[k]).wait()

    def receive_dots(k, count):
        wait_dots(dot_recv, k)
        row = msg[k] + jnp.sum(dots_in[k], axis=0)
        return [row[:, i : i + 1] for i in range(count)]

    for copy in loads:
        copy.wait()
    start = place * own
    total_nodes = own * places
    diagonal = mass_ref[0]
    here = start + lax.broadcasted_iota(jnp.int32, (1, own), 1)
    for d in range(degree):
        used = nbr_ref[0, d : d + 1, :] != here
        diagonal = diagonal + jnp.where(used, mean_ref[0, d : d + 1, :], 0.0)
    last = ITERS // 2

    first_row = lax.broadcasted_iota(jnp.int32, (half, own), 0) == 0

    def prepare(where_to, ripple, mean, spot, hot):
        height = hot.shape[0]
        row_index = lax.broadcasted_iota(jnp.int32, (height, own), 0)
        for d in range(degree):
            spectrum = dot_high(plain_ref[...], ripple(d))
            real, imag = spectrum[:half], spectrum[half:]
            k_re[where_to, d] = real + mean(d)
            k_re2[where_to, d] = jnp.where(first_row, imag, real) + mean(d)
            k_im[where_to, d] = jnp.where(first_row, 0.0, imag)
            hot[:, d * own : (d + 1) * own] = jnp.where(row_index == spot(d), 1.0, 0.0).astype(jnp.bfloat16)

    prepare(
        0,
        lambda d: rip_ref[0, :, d, :],
        lambda d: mean_ref[0, d : d + 1, :],
        lambda d: jnp.bitwise_and(nbr_ref[0, d : d + 1, :] - start, own2 - 1),
        hot_own,
    )
    outward = jnp.where(lax.broadcasted_iota(jnp.int32, (half, own), 1) < IF, 0, 1) == side
    for d in range(degree):
        folded = pltpu.roll(rip_ref[0, half:, d, :], IF, 1)
        packed[0, :, d, :] = jnp.where(outward, rip_ref[0, :half, d, :], folded)
    outgoing = [(source.at[0], target.at[2]) for source, target in (
        (nbr_ref, nbr_ref), (mean_ref, mean_ref), (mass_ref, mass_ref), (eddy_ref, eddy_ref)
    )] + [(packed.at[0], packed.at[1])]

    pl.semaphore_wait(barrier, places - 1 + len(extra))

    rhs_copies = []
    for o in range(1, n_harm):
        peer = lax.rem(h + o, n_harm)
        copy = pltpu.make_async_remote_copy(
            src_ref=rhs_ref.at[:, lanes(side_of(peer, s))],
            dst_ref=rhs_all.at[rows(h)],
            send_sem=rhs_send.at[o - 1],
            recv_sem=rhs_recv.at[o - 1],
            device_id=(peer, s),
            device_id_type=MESH,
        )
        copy.start()
        rhs_copies.append(copy)
    cross = device_at(lax.rem(place + places + 2 * side - 1, places))
    cross_copies = []
    for i, (source, target) in enumerate(outgoing):
        copy = pltpu.make_async_remote_copy(
            src_ref=source,
            dst_ref=target,
            send_sem=cross_send.at[i],
            recv_sem=cross_recv.at[i],
            device_id=cross,
            device_id_type=MESH,
        )
        copy.start()
        cross_copies.append(copy)

    for copy in rhs_copies:
        copy.wait_recv()
    field[0] = dot_high(unit_ref[...], rhs_all[...])
    send_halo(0, field.at[0])
    send_dots(last, [diagonal])
    for copy in cross_copies:
        copy.wait_recv()
    lane_full = lax.broadcasted_iota(jnp.int32, (harmonics, own), 1)
    from_partner = jnp.where(lane_full < IF, 0, 1) == side

    def ghost(ref, index):
        partner, outer = ref[(1, *index)], ref[(2, *index)]
        return jnp.where(from_partner[: partner.shape[0]], partner, outer)

    def ghost_ripple(d):
        low = packed[1, :, d, :]
        outer = jnp.concatenate([low, pltpu.roll(low, IF, 1)], axis=0)
        return jnp.where(from_partner, rip_ref[1, :, d, :], outer)

    def ghost_spot(d):
        place_of = ghost(nbr_ref, (slice(d, d + 1), slice(None))) - start
        place_of = jnp.where(place_of < 0, place_of + total_nodes, place_of)
        return jnp.where(place_of >= total_nodes - own, place_of - (total_nodes - 3 * own), place_of)

    prepare(
        1,
        ghost_ripple,
        lambda d: ghost(mean_ref, (slice(d, d + 1), slice(None))),
        ghost_spot,
        hot_ghost,
    )
    whole_row = (slice(None), slice(None))
    wait_dots(dot_recv, last)
    theta = jnp.sum(msg[last] + jnp.sum(dots_in[last], axis=0), axis=1, keepdims=True) / total_nodes
    mass = [mass_ref[0] - theta, ghost(mass_ref, whole_row) - theta]
    eddy = [eddy_ref[0], ghost(eddy_ref, whole_row)]

    def stack(*tiles):
        pieces = [split_parts(tile, 3) for tile in tiles]
        return jnp.concatenate([jnp.concatenate(row, axis=1) for row in zip(*pieces)], axis=0)

    def operate(which, vector, stacked, hot):
        high, low = split_parts(vector, 2)
        swapped = jnp.dot(
            swap_ref[...], jnp.concatenate([high, high, low, low], axis=0),
            preferred_element_type=jnp.float32,
        )
        total = mass[which] * vector + eddy[which] * swapped
        v_re, v_im = vector[:half], vector[half:]
        sum_re, sum_im = total[:half], total[half:]
        for d in range(0, degree, 2):
            far = jnp.dot(stacked, hot[:, d * own : (d + 2) * own], preferred_element_type=jnp.float32)
            far = far[:harmonics] + far[harmonics : 2 * harmonics] + far[2 * harmonics :]
            for e in range(2):
                g_re = v_re - far[:half, e * own : (e + 1) * own]
                g_im = v_im - far[half:, e * own : (e + 1) * own]
                re, re2, im = k_re[which, d + e], k_re2[which, d + e], k_im[which, d + e]
                sum_re += re * g_re - im * g_im
                sum_im += re2 * g_im + im * g_re
        return jnp.concatenate([sum_re, sum_im], axis=0)

    def operate_twice(k, vector):
        halo_copies[2 * k].wait_recv()
        halo_copies[2 * k + 1].wait_recv()
        before, after = halo[k, 0], halo[k, 1]
        outer = jnp.where(near, after, before)
        once = operate(0, vector, stack(vector, outer), hot_own)
        once_outer = operate(1, outer, stack(vector, after, before), hot_ghost)
        return once, operate(0, once, stack(once, once_outer), hot_own)

    rhs = field[0]
    first, second = operate_twice(0, rhs)
    field[1] = second
    send_halo(1, field.at[1])
    send_dots(0, [rhs * rhs, rhs * first, rhs * second, first * first, first * second, second * second])
    third, fourth = operate_twice(1, second)
    rr, *found = receive_dots(0, 6)
    per_rr = 1.0 / rr
    beta = jnp.sqrt(rr)
    inverse = 1.0 / beta
    basis[0] = rhs * inverse
    image[0] = first * inverse
    image2[0] = second * inverse
    third, fourth = third * inverse, fourth * inverse
    found = [value * per_rr for value in found]
    fit = LeastSquares(beta)
    shifted = []
    pending = []

    def flush():
        for column in pending:
            i = len(fit.triangle)
            fit.add(column[:i] + [column[i] + theta] + column[i + 1 :])
        pending.clear()

    for m in range(0, ITERS, 2):
        on_more = m + 2 < ITERS
        x1, x2 = image[m], image2[m]
        if m > 0:
            if on_more:
                send_halo(m // 2 + 1, image2.at[m])
            kept = [basis[i] for i in range(m + 1)]
            send_dots(
                m // 2,
                [v * x1 for v in kept] + [v * x2 for v in kept] + [x1 * x1, x1 * x2, x2 * x2],
            )
            if on_more:
                third, fourth = operate_twice(m // 2 + 1, x2)
            flush()
            found = receive_dots(m // 2, 2 * m + 5)
        dot1, dot2 = found[: m + 1], found[m + 1 : 2 * m + 2]
        s11, s12, s22 = found[2 * m + 2 :]
        for p, q in zip(dot1, dot2):
            s11, s12, s22 = s11 - p * p, s12 - p * q, s22 - q * q
        length1 = jnp.sqrt(s11)
        scale1 = 1.0 / length1
        dot2.append(s12 * scale1)
        length2 = jnp.sqrt(s22 - dot2[-1] * dot2[-1])
        scale2 = 1.0 / length2
        column = dot1 + [length1]
        shifted.append(column)
        pending.append(column)
        column = dot2 + [length2]
        for i, value in enumerate(dot1):
            for k, entry in enumerate(shifted[i]):
                column[k] = column[k] - value * entry
        column = [entry * scale1 for entry in column]
        shifted.append(column)
        pending.append(column)
        new_v, new_p = x1, x2
        for i, value in enumerate(dot1):
            new_v = new_v - value * basis[i]
            new_p = new_p - value * image[i]
        basis[m + 1] = new_v * scale1
        image[m + 1] = new_p * scale1
        if on_more:
            new_q = third
            for i, value in enumerate(dot1):
                new_q = new_q - value * image2[i]
            image2[m + 1] = new_q * scale1
            new_v, new_p, new_q = x2, third, fourth
            for i, value in enumerate(dot2):
                new_v = new_v - value * basis[i]
                new_p = new_p - value * image[i]
                new_q = new_q - value * image2[i]
            basis[m + 2] = new_v * scale2
            image[m + 2] = new_p * scale2
            image2[m + 2] = new_q * scale2
    flush()
    coeffs = fit.solve()
    correction = coeffs[0] * basis[0]
    product = coeffs[0] * image[0]
    for j in range(1, ITERS):
        correction = correction + coeffs[j] * basis[j]
        product = product + coeffs[j] * image[j]
    residual = rhs - product - theta * correction
    phys[0] = dot_high(unit_t_ref[...], correction)
    phys[1] = dot_high(unit_t_ref[...], residual)

    other = lax.rem(h + group, n_harm)
    final = pltpu.make_async_remote_copy(
        src_ref=phys.at[:, rows(other)],
        dst_ref=phys_in,
        send_sem=out_send,
        recv_sem=out_recv,
        device_id=(other, s),
        device_id_type=MESH,
    )
    final.start()
    corr_ref[:, lanes(side)] = phys[0, rows(h)]
    res_ref[:, lanes(side)] = phys[1, rows(h)]
    for copy in rhs_copies + cross_copies + halo_copies:
        copy.wait_send()
    for k in range(ITERS // 2 + 1):
        wait_dots(dot_send, k)
    final.wait()
    corr_ref[:, lanes(1 - side)] = phys_in[0]
    res_ref[:, lanes(1 - side)] = phys_in[1]


def per_device(n_harm, n_space, rhs_field, neighbors, nu_mean, nu_ripple, mass_coeff, eddy_coeff):
    block, own2 = rhs_field.shape
    own = own2 // 2
    harmonics, degree = nu_ripple.shape[:2]
    plain, unit, unit_t, swap_parts = tables(harmonics)
    places = 2 * n_space
    f32 = jnp.float32
    vmem = pl.BlockSpec(memory_space=pltpu.VMEM)
    dma = pltpu.SemaphoreType.DMA
    return pl.pallas_call(
        functools.partial(gmres_kernel, n_harm, n_space),
        out_shape=(jax.ShapeDtypeStruct((block, own2), f32),) * 2,
        in_specs=[pl.BlockSpec(memory_space=pltpu.HBM)] * 10,
        out_specs=(vmem, vmem),
        scratch_shapes=[
            pltpu.VMEM((3, degree, own), neighbors.dtype),
            pltpu.VMEM((3, degree, own), f32),
            pltpu.VMEM((2, harmonics, degree, own), f32),
            pltpu.VMEM((3, 1, own), f32),
            pltpu.VMEM((3, 1, own), f32),
            pltpu.VMEM((harmonics, harmonics), f32),
            pltpu.VMEM((harmonics, harmonics), f32),
            pltpu.VMEM((harmonics, harmonics), f32),
            pltpu.VMEM(swap_parts.shape, jnp.bfloat16),
            dma((15,)),
            pltpu.VMEM((2, harmonics // 2, degree, own), f32),
            dma((5,)),
            dma((5,)),
            pltpu.VMEM((harmonics, own), f32),
            pltpu.VMEM((own2, degree * own), jnp.bfloat16),
            pltpu.VMEM((3 * own, degree * own), jnp.bfloat16),
            pltpu.VMEM((2, degree, harmonics // 2, own), f32),
            pltpu.VMEM((2, degree, harmonics // 2, own), f32),
            pltpu.VMEM((2, degree, harmonics // 2, own), f32),
            pltpu.VMEM((ITERS, harmonics, own), f32),
            pltpu.VMEM((ITERS, harmonics, own), f32),
            pltpu.VMEM((ITERS, harmonics, own), f32),
            pltpu.VMEM((2, harmonics, own), f32),
            pltpu.VMEM((ITERS // 2, 2, harmonics, own), f32),
            pltpu.VMEM((ITERS // 2 + 1, 1, 128), f32),
            pltpu.VMEM((ITERS // 2 + 1, places - 1, 1, 128), f32),
            pltpu.VMEM((2, harmonics, own), f32),
            pltpu.VMEM((2, block, own), f32),
            dma((n_harm - 1,)),
            dma((n_harm - 1,)),
            dma((ITERS // 2, 2)),
            dma((ITERS // 2, 2)),
            dma((ITERS // 2 + 1,)),
            dma((ITERS // 2 + 1,)),
            dma,
            dma,
        ],
        compiler_params=pltpu.CompilerParams(
            collective_id=0, has_side_effects=True, vmem_limit_bytes=60 * 1024 * 1024
        ),
    )(
        rhs_field, neighbors, nu_mean, nu_ripple,
        mass_coeff.reshape(1, own2), eddy_coeff.reshape(1, own2),
        jnp.asarray(plain), jnp.asarray(unit), jnp.asarray(unit_t), jnp.asarray(swap_parts),
    )


def solution(mesh):
    return jax.shard_map(
        functools.partial(per_device, mesh.shape["harm"], mesh.shape["space"]),
        mesh=mesh,
        in_specs=(
            P("harm", "space"),
            P(None, "space"),
            P(None, "space"),
            P(None, None, "space"),
            P("space"),
            P("space"),
        ),
        out_specs=(P("harm", "space"), P("harm", "space")),
        check_vma=False,
    )
```

```python
import functools

import jax
import jax.numpy as jnp
import ml_dtypes
import numpy as np
from jax import lax
from jax.experimental import pallas as pl
from jax.experimental.pallas import tpu as pltpu
from jax.sharding import PartitionSpec as P

IF = 64
ITERS = 8
MESH = pl.DeviceIdType.MESH


def tables(harmonics):
    half = harmonics // 2
    index = np.arange(harmonics)
    phase = 2.0 * np.pi * ((index[:, None] * index[None, :]) % harmonics) / harmonics
    plain = np.concatenate([np.cos(phase[:half]), -np.sin(phase[:half])], axis=0)
    plain[half] = np.cos(phase[half])
    scale = np.full((harmonics, 1), np.sqrt(2.0 / harmonics))
    scale[0] = scale[half] = np.sqrt(1.0 / harmonics)
    unitary = plain * scale
    swap = np.zeros((harmonics, harmonics))
    swap[index, index ^ 1] = 4.0 * (index // 2 + 1) / harmonics * np.where(index % 2 == 0, 1.0, -1.0)
    swap = unitary @ swap @ unitary.T
    high = swap.astype(np.float32).astype(ml_dtypes.bfloat16)
    low = (swap - high.astype(np.float64)).astype(ml_dtypes.bfloat16)
    swap_parts = np.concatenate([high, low, high, low], axis=1)
    return plain.astype(np.float32), unitary.astype(np.float32), unitary.T.astype(np.float32), swap_parts


def split_parts(value, count):
    parts = []
    for _ in range(count):
        part = value.astype(jnp.bfloat16)
        parts.append(part)
        value = value - part.astype(jnp.float32)
    return parts


def dot_high(left, right):
    return jnp.dot(left, right, precision=lax.Precision.HIGHEST, preferred_element_type=jnp.float32)


class LeastSquares:
    def __init__(self, beta):
        self.rotations = []
        self.triangle = []
        self.target = [beta]

    def add(self, column):
        col = list(column)
        for i, (cosine, sine) in enumerate(self.rotations):
            first, second = col[i], col[i + 1]
            col[i] = cosine * first + sine * second
            col[i + 1] = cosine * second - sine * first
        j = len(self.rotations)
        radius = jnp.sqrt(col[j] * col[j] + col[j + 1] * col[j + 1])
        cosine, sine = col[j] / radius, col[j + 1] / radius
        self.rotations.append((cosine, sine))
        col[j] = radius
        self.target.append(-sine * self.target[j])
        self.target[j] = cosine * self.target[j]
        self.triangle.append(col[: j + 1])

    def solve(self):
        steps = len(self.triangle)
        coeffs = [None] * steps
        for j in reversed(range(steps)):
            running = self.target[j]
            for k in range(j + 1, steps):
                running = running - self.triangle[k][j] * coeffs[k]
            coeffs[j] = running / self.triangle[j][j]
        return coeffs


def gmres_kernel(
    n_harm, n_space,
    rhs_ref, nbr_hbm, mean_hbm, rip_hbm, mass_hbm, eddy_hbm,
    plain_hbm, unit_hbm, unit_t_hbm, swap_hbm,
    corr_ref, res_ref,
    nbr_ref, mean_ref, rip_ref, mass_ref, eddy_ref, plain_ref, unit_ref, unit_t_ref, swap_ref, load_sem,
    packed, cross_send, cross_recv,
    rhs_all, hot_own, hot_ghost, k_re, k_re2, k_im, basis, image, image2, field, halo, msg, dots_in, phys, phys_in,
    rhs_send, rhs_recv, halo_send, halo_recv, dot_send, dot_recv, out_send, out_recv,
):
    block, own2 = rhs_ref.shape
    own = own2 // 2
    harmonics = rip_hbm.shape[0]
    half = harmonics // 2
    degree = nbr_hbm.shape[0]
    group = n_harm // 2
    places = 2 * n_space
    h = lax.axis_index("harm")
    s = lax.axis_index("space")
    lane_rank = lax.rem(h, group)

    def side_of(harm, space):
        return lax.rem(harm // group + space, 2)

    side = side_of(h, s)
    place = 2 * s + side

    def device_at(position):
        space = lax.shift_right_logical(position, 1)
        return (jnp.bitwise_and(position + space, 1) * group + lane_rank, space)

    def around(offset):
        position = place + offset
        return device_at(jnp.where(position >= places, position - places, position))

    def lanes(which):
        return pl.ds(pl.multiple_of(which * own, own), own)

    def rows(which):
        return pl.ds(pl.multiple_of(which * block, block), block)

    edge_data = (
        (nbr_hbm, nbr_ref), (mean_hbm, mean_ref), (mass_hbm, mass_ref), (rip_hbm, rip_ref), (eddy_hbm, eddy_ref)
    )
    loads = []

    def load(source, target):
        copy = pltpu.make_async_copy(source, target, load_sem.at[len(loads)])
        copy.start()
        loads.append(copy)

    def part(source, which):
        return source.at[:, :, lanes(which)] if len(source.shape) == 3 else source.at[:, lanes(which)]

    for source, target in edge_data:
        load(part(source, side), target.at[0])
    load(plain_hbm, plain_ref)
    load(rhs_ref.at[:, lanes(side)], rhs_all.at[rows(h)])
    load(unit_hbm, unit_ref)
    load(swap_hbm, swap_ref)
    load(unit_t_hbm, unit_t_ref)
    for source, target in edge_data:
        load(part(source, 1 - side), target.at[1])

    barrier = pltpu.get_barrier_semaphore()

    def greet(offset, carry):
        pl.semaphore_signal(barrier, inc=1, device_id=around(offset), device_id_type=MESH)
        return carry

    lax.fori_loop(1, places, greet, 0)
    extra = [o for o in range(1, n_harm) if o % group != 0]
    for o in extra:
        pl.semaphore_signal(barrier, inc=1, device_id=(lax.rem(h + o, n_harm), s), device_id_type=MESH)

    lane_index = lax.broadcasted_iota(jnp.int32, (1, 128), 1)
    near = lax.broadcasted_iota(jnp.int32, (harmonics, own), 1) < IF
    left = device_at(lax.rem(place + places - 1, places))
    right = device_at(lax.rem(place + 1, places))
    halo_copies = []

    def send_halo(k, source):
        for way, target in ((0, right), (1, left)):
            copy = pltpu.make_async_remote_copy(
                src_ref=source,
                dst_ref=halo.at[k, way],
                send_sem=halo_send.at[k, way],
                recv_sem=halo_recv.at[k, way],
                device_id=target,
                device_id_type=MESH,
            )
            copy.start()
            halo_copies.append(copy)

    def total_of(product):
        return jnp.sum(jnp.sum(product, axis=0, keepdims=True), axis=1, keepdims=True)

    def send_dots(k, products):
        row = jnp.zeros((1, 128), jnp.float32)
        for i, product in enumerate(products):
            row = jnp.where(lane_index == i, total_of(product), row)
        msg[k] = row

        def send(step, carry):
            offset = places - step
            pltpu.make_async_remote_copy(
                src_ref=msg.at[k],
                dst_ref=dots_in.at[k, offset - 1],
                send_sem=dot_send.at[k],
                recv_sem=dot_recv.at[k],
                device_id=device_at(jnp.bitwise_xor(place, offset)),
                device_id_type=MESH,
            ).start()
            return carry

        lax.fori_loop(1, places, send, 0)

    def wait_dots(sem, k):
        pltpu.make_async_copy(dots_in.at[k], dots_in.at[k], sem.at[k]).wait()

    def receive_dots(k, count):
        wait_dots(dot_recv, k)
        row = msg[k] + jnp.sum(dots_in[k], axis=0)
        return [row[:, i : i + 1] for i in range(count)]

    for copy in loads:
        copy.wait()
    start = place * own
    total_nodes = own * places
    diagonal = mass_ref[0]
    here = start + lax.broadcasted_iota(jnp.int32, (1, own), 1)
    for d in range(degree):
        used = nbr_ref[0, d : d + 1, :] != here
        diagonal = diagonal + jnp.where(used, mean_ref[0, d : d + 1, :], 0.0)
    last = ITERS // 2

    first_row = lax.broadcasted_iota(jnp.int32, (half, own), 0) == 0

    def prepare(where_to, ripple, mean, spot, hot):
        height = hot.shape[0]
        row_index = lax.broadcasted_iota(jnp.int32, (height, own), 0)
        for d in range(degree):
            spectrum = dot_high(plain_ref[...], ripple(d))
            real, imag = spectrum[:half], spectrum[half:]
            k_re[where_to, d] = real + mean(d)
            k_re2[where_to, d] = jnp.where(first_row, imag, real) + mean(d)
            k_im[where_to, d] = jnp.where(first_row, 0.0, imag)
            hot[:, d * own : (d + 1) * own] = jnp.where(row_index == spot(d), 1.0, 0.0).astype(jnp.bfloat16)

    prepare(
        0,
        lambda d: rip_ref[0, :, d, :],
        lambda d: mean_ref[0, d : d + 1, :],
        lambda d: jnp.bitwise_and(nbr_ref[0, d : d + 1, :] - start, own2 - 1),
        hot_own,
    )
    outward = jnp.where(lax.broadcasted_iota(jnp.int32, (half, own), 1) < IF, 0, 1) == side
    for d in range(degree):
        folded = pltpu.roll(rip_ref[0, half:, d, :], IF, 1)
        packed[0, :, d, :] = jnp.where(outward, rip_ref[0, :half, d, :], folded)
    outgoing = [(source.at[0], target.at[2]) for source, target in (
        (nbr_ref, nbr_ref), (mean_ref, mean_ref), (mass_ref, mass_ref), (eddy_ref, eddy_ref)
    )] + [(packed.at[0], packed.at[1])]

    pl.semaphore_wait(barrier, places - 1 + len(extra))

    rhs_copies = []
    for o in range(1, n_harm):
        peer = lax.rem(h + o, n_harm)
        copy = pltpu.make_async_remote_copy(
            src_ref=rhs_ref.at[:, lanes(side_of(peer, s))],
            dst_ref=rhs_all.at[rows(h)],
            send_sem=rhs_send.at[o - 1],
            recv_sem=rhs_recv.at[o - 1],
            device_id=(peer, s),
            device_id_type=MESH,
        )
        copy.start()
        rhs_copies.append(copy)
    cross = device_at(lax.rem(place + places + 2 * side - 1, places))
    cross_copies = []
    for i, (source, target) in enumerate(outgoing):
        copy = pltpu.make_async_remote_copy(
            src_ref=source,
            dst_ref=target,
            send_sem=cross_send.at[i],
            recv_sem=cross_recv.at[i],
            device_id=cross,
            device_id_type=MESH,
        )
        copy.start()
        cross_copies.append(copy)

    for copy in rhs_copies:
        copy.wait_recv()
    field[0] = dot_high(unit_ref[...], rhs_all[...])
    send_halo(0, field.at[0])
    send_dots(last, [diagonal])
    for copy in cross_copies:
        copy.wait_recv()
    lane_full = lax.broadcasted_iota(jnp.int32, (harmonics, own), 1)
    from_partner = jnp.where(lane_full < IF, 0, 1) == side

    def ghost(ref, index):
        partner, outer = ref[(1, *index)], ref[(2, *index)]
        return jnp.where(from_partner[: partner.shape[0]], partner, outer)

    def ghost_ripple(d):
        low = packed[1, :, d, :]
        outer = jnp.concatenate([low, pltpu.roll(low, IF, 1)], axis=0)
        return jnp.where(from_partner, rip_ref[1, :, d, :], outer)

    def ghost_spot(d):
        place_of = ghost(nbr_ref, (slice(d, d + 1), slice(None))) - start
        place_of = jnp.where(place_of < 0, place_of + total_nodes, place_of)
        return jnp.where(place_of >= total_nodes - own, place_of - (total_nodes - 3 * own), place_of)

    prepare(
        1,
        ghost_ripple,
        lambda d: ghost(mean_ref, (slice(d, d + 1), slice(None))),
        ghost_spot,
        hot_ghost,
    )
    whole_row = (slice(None), slice(None))
    wait_dots(dot_recv, last)
    theta = jnp.sum(msg[last] + jnp.sum(dots_in[last], axis=0), axis=1, keepdims=True) / total_nodes
    mass = [mass_ref[0] - theta, ghost(mass_ref, whole_row) - theta]
    eddy = [eddy_ref[0], ghost(eddy_ref, whole_row)]

    def stack(*tiles):
        pieces = [split_parts(tile, 3) for tile in tiles]
        return jnp.concatenate([jnp.concatenate(row, axis=1) for row in zip(*pieces)], axis=0)

    def operate(which, vector, stacked, hot):
        high, low = split_parts(vector, 2)
        swapped = jnp.dot(
            swap_ref[...], jnp.concatenate([high, high, low, low], axis=0),
            preferred_element_type=jnp.float32,
        )
        total = mass[which] * vector + eddy[which] * swapped
        v_re, v_im = vector[:half], vector[half:]
        sum_re, sum_im = total[:half], total[half:]
        for d in range(0, degree, 2):
            far = jnp.dot(stacked, hot[:, d * own : (d + 2) * own], preferred_element_type=jnp.float32)
            far = far[:harmonics] + far[harmonics : 2 * harmonics] + far[2 * harmonics :]
            for e in range(2):
                g_re = v_re - far[:half, e * own : (e + 1) * own]
                g_im = v_im - far[half:, e * own : (e + 1) * own]
                re, re2, im = k_re[which, d + e], k_re2[which, d + e], k_im[which, d + e]
                sum_re += re * g_re - im * g_im
                sum_im += re2 * g_im + im * g_re
        return jnp.concatenate([sum_re, sum_im], axis=0)

    def operate_twice(k, vector):
        halo_copies[2 * k].wait_recv()
        halo_copies[2 * k + 1].wait_recv()
        before, after = halo[k, 0], halo[k, 1]
        outer = jnp.where(near, after, before)
        once = operate(0, vector, stack(vector, outer), hot_own)
        once_outer = operate(1, outer, stack(vector, after, before), hot_ghost)
        return once, operate(0, once, stack(once, once_outer), hot_own)

    rhs = field[0]
    first, second = operate_twice(0, rhs)
    field[1] = second
    send_halo(1, field.at[1])
    send_dots(0, [rhs * rhs, rhs * first, rhs * second, first * first, first * second, second * second])
    third, fourth = operate_twice(1, second)
    rr, *found = receive_dots(0, 6)
    per_rr = 1.0 / rr
    beta = jnp.sqrt(rr)
    inverse = 1.0 / beta
    basis[0] = rhs * inverse
    image[0] = first * inverse
    image2[0] = second * inverse
    third, fourth = third * inverse, fourth * inverse
    found = [value * per_rr for value in found]
    fit = LeastSquares(beta)
    shifted = []
    pending = []

    def flush():
        for column in pending:
            i = len(fit.triangle)
            fit.add(column[:i] + [column[i] + theta] + column[i + 1 :])
        pending.clear()

    for m in range(0, ITERS, 2):
        on_more = m + 2 < ITERS
        x1, x2 = image[m], image2[m]
        if m > 0:
            if on_more:
                send_halo(m // 2 + 1, image2.at[m])
            kept = [basis[i] for i in range(m + 1)]
            send_dots(
                m // 2,
                [v * x1 for v in kept] + [v * x2 for v in kept] + [x1 * x1, x1 * x2, x2 * x2],
            )
            if on_more:
                third, fourth = operate_twice(m // 2 + 1, x2)
            flush()
            found = receive_dots(m // 2, 2 * m + 5)
        dot1, dot2 = found[: m + 1], found[m + 1 : 2 * m + 2]
        s11, s12, s22 = found[2 * m + 2 :]
        for p, q in zip(dot1, dot2):
            s11, s12, s22 = s11 - p * p, s12 - p * q, s22 - q * q
        length1 = jnp.sqrt(s11)
        scale1 = 1.0 / length1
        dot2.append(s12 * scale1)
        length2 = jnp.sqrt(s22 - dot2[-1] * dot2[-1])
        scale2 = 1.0 / length2
        column = dot1 + [length1]
        shifted.append(column)
        pending.append(column)
        column = dot2 + [length2]
        for i, value in enumerate(dot1):
            for k, entry in enumerate(shifted[i]):
                column[k] = column[k] - value * entry
        column = [entry * scale1 for entry in column]
        shifted.append(column)
        pending.append(column)
        new_v, new_p = x1, x2
        for i, value in enumerate(dot1):
            new_v = new_v - value * basis[i]
            new_p = new_p - value * image[i]
        basis[m + 1] = new_v * scale1
        image[m + 1] = new_p * scale1
        if on_more:
            new_q = third
            for i, value in enumerate(dot1):
                new_q = new_q - value * image2[i]
            image2[m + 1] = new_q * scale1
            new_v, new_p, new_q = x2, third, fourth
            for i, value in enumerate(dot2):
                new_v = new_v - value * basis[i]
                new_p = new_p - value * image[i]
                new_q = new_q - value * image2[i]
            basis[m + 2] = new_v * scale2
            image[m + 2] = new_p * scale2
            image2[m + 2] = new_q * scale2
    flush()
    coeffs = fit.solve()
    correction = coeffs[0] * basis[0]
    product = coeffs[0] * image[0]
    for j in range(1, ITERS):
        correction = correction + coeffs[j] * basis[j]
        product = product + coeffs[j] * image[j]
    residual = rhs - product - theta * correction
    phys[0] = dot_high(unit_t_ref[...], correction)
    phys[1] = dot_high(unit_t_ref[...], residual)

    other = lax.rem(h + group, n_harm)
    final = pltpu.make_async_remote_copy(
        src_ref=phys.at[:, rows(other)],
        dst_ref=phys_in,
        send_sem=out_send,
        recv_sem=out_recv,
        device_id=(other, s),
        device_id_type=MESH,
    )
    final.start()
    corr_ref[:, lanes(side)] = phys[0, rows(h)]
    res_ref[:, lanes(side)] = phys[1, rows(h)]
    for copy in rhs_copies + cross_copies + halo_copies:
        copy.wait_send()
    for k in range(ITERS // 2 + 1):
        wait_dots(dot_send, k)
    final.wait()
    corr_ref[:, lanes(1 - side)] = phys_in[0]
    res_ref[:, lanes(1 - side)] = phys_in[1]


def per_device(n_harm, n_space, rhs_field, neighbors, nu_mean, nu_ripple, mass_coeff, eddy_coeff):
    block, own2 = rhs_field.shape
    own = own2 // 2
    harmonics, degree = nu_ripple.shape[:2]
    plain, unit, unit_t, swap_parts = tables(harmonics)
    places = 2 * n_space
    f32 = jnp.float32
    vmem = pl.BlockSpec(memory_space=pltpu.VMEM)
    dma = pltpu.SemaphoreType.DMA
    return pl.pallas_call(
        functools.partial(gmres_kernel, n_harm, n_space),
        out_shape=(jax.ShapeDtypeStruct((block, own2), f32),) * 2,
        in_specs=[pl.BlockSpec(memory_space=pltpu.HBM)] * 10,
        out_specs=(vmem, vmem),
        scratch_shapes=[
            pltpu.VMEM((3, degree, own), neighbors.dtype),
            pltpu.VMEM((3, degree, own), f32),
            pltpu.VMEM((2, harmonics, degree, own), f32),
            pltpu.VMEM((3, 1, own), f32),
            pltpu.VMEM((3, 1, own), f32),
            pltpu.VMEM((harmonics, harmonics), f32),
            pltpu.VMEM((harmonics, harmonics), f32),
            pltpu.VMEM((harmonics, harmonics), f32),
            pltpu.VMEM(swap_parts.shape, jnp.bfloat16),
            dma((15,)),
            pltpu.VMEM((2, harmonics // 2, degree, own), f32),
            dma((5,)),
            dma((5,)),
            pltpu.VMEM((harmonics, own), f32),
            pltpu.VMEM((own2, degree * own), jnp.bfloat16),
            pltpu.VMEM((3 * own, degree * own), jnp.bfloat16),
            pltpu.VMEM((2, degree, harmonics // 2, own), f32),
            pltpu.VMEM((2, degree, harmonics // 2, own), f32),
            pltpu.VMEM((2, degree, harmonics // 2, own), f32),
            pltpu.VMEM((ITERS, harmonics, own), f32),
            pltpu.VMEM((ITERS, harmonics, own), f32),
            pltpu.VMEM((ITERS, harmonics, own), f32),
            pltpu.VMEM((2, harmonics, own), f32),
            pltpu.VMEM((ITERS // 2, 2, harmonics, own), f32),
            pltpu.VMEM((ITERS // 2 + 1, 1, 128), f32),
            pltpu.VMEM((ITERS // 2 + 1, places - 1, 1, 128), f32),
            pltpu.VMEM((2, harmonics, own), f32),
            pltpu.VMEM((2, block, own), f32),
            dma((n_harm - 1,)),
            dma((n_harm - 1,)),
            dma((ITERS // 2, 2)),
            dma((ITERS // 2, 2)),
            dma((ITERS // 2 + 1,)),
            dma((ITERS // 2 + 1,)),
            dma,
            dma,
        ],
        compiler_params=pltpu.CompilerParams(
            collective_id=0, has_side_effects=True, vmem_limit_bytes=60 * 1024 * 1024
        ),
    )(
        rhs_field, neighbors, nu_mean, nu_ripple,
        mass_coeff.reshape(1, own2), eddy_coeff.reshape(1, own2),
        jnp.asarray(plain), jnp.asarray(unit), jnp.asarray(unit_t), jnp.asarray(swap_parts),
    )


def solution(mesh):
    return jax.shard_map(
        functools.partial(per_device, mesh.shape["harm"], mesh.shape["space"]),
        mesh=mesh,
        in_specs=(
            P("harm", "space"),
            P(None, "space"),
            P(None, "space"),
            P(None, None, "space"),
            P("space"),
            P("space"),
        ),
        out_specs=(P("harm", "space"), P("harm", "space")),
        check_vma=False,
    )
```
